32 devices in a mesh: groups: 2 (over y), col: 4 (over z), row: 4 (over x, core).
Axes of the slice: x: 2, y: 2, z: 4, core: 2. Of those that a mesh axis runs over, the one named last changes fastest.
Arguments:
- pair_slab: bfloat16 [128, 512, 128], P(('groups', 'row'), 'col'), parts along dimension 0, may hold values from -6 to 6
- tile_pair: bfloat16 [8, 2, 128, 128, 128], P(('groups', 'col'), None, 'row'), parts along dimension 0, may hold values from -6 to 6
- tile_cotan: bfloat16 [8, 2, 128, 128, 128], P(('groups', 'col'), None, 'row'), parts along dimension 0, may hold values from -6 to 6
- tile_rows: int32 [8, 2], P(('groups', 'col')), parts along dimension 0, may hold values from 0 to 3, as said below
- tile_count: int32 [8], P(('groups', 'col')), parts along dimension 0, may hold values from 1 to 2, as said below
- norm_gain: float32 [128], replicated, may hold values from 0.5 to 1.5
- norm_bias: float32 [128], replicated, may hold values from -2.5 to 2.5
- w_in: bfloat16 [128, 512], replicated, may hold values from -0.5 to 0.5
- out_gain: float32 [128], replicated, may hold values from 0.5 to 1.5
- out_bias: float32 [128], replicated, may hold values from -2.5 to 2.5
- w_out: bfloat16 [128, 128], replicated, may hold values from -0.5 to 0.5
- w_gate: bfloat16 [128, 128], replicated, may hold values from -0.5 to 0.5
Outputs:
- update: bfloat16 [8, 2, 128, 128, 128], P(('groups', 'col'), None, 'row'), parts along dimension 0
- grad_slab: bfloat16 [128, 512, 128], P(('groups', 'row'), 'col'), parts along dimension 0
- grad_tiles: bfloat16 [8, 2, 128, 128, 128], P(('groups', 'col'), None, 'row'), parts along dimension 0
- grad_in_w: float32 [256, 512], P('groups'), parts along dimension 0
- grad_out_w: float32 [256, 128], P('groups'), parts along dimension 0
- grad_gate_w: float32 [256, 128], P('groups'), parts along dimension 0
The draws below stay inside these ranges and needn't reach their ends.
There are 2 independent parts, one for each index of `groups`. The reference program is written for one: setup_inputs(seed, part) draws one part's arguments, and reference() takes and returns one part's arrays. A program takes and returns all parts, laid end to end along the dimension named above; an argument that names none is the same for every part. Nothing has to cross between parts.
Inputs may be any that keep to these rules, and one draw needn't show every extreme that they name: `tile_count`: every column block has at least one active slot and some column block has all 2 active. `tile_rows`: the row blocks named by the slots of one column block are distinct; slots at or past the count are inactive.
All inputs are finite; a program needn't handle non-finite values.
Results may differ from the reference program's by a relative error of at most 0.015.
Values may be sent and summed in bfloat16 or wider, within the bound.
A program may use at most 128 MiB of HBM per device.

```python
import jax
import jax.numpy as jnp
from jax import lax

C = 128
H = 128
TILE = 128
K_DEV = 16
SLOTS = 2
K = 64
BLOCKS = 4
N = 512
N_ROW = 4


def draw_tile_count(key, part):
    counts = jax.random.randint(key, (BLOCKS,), 1, SLOTS + 1)
    where = jax.random.randint(jax.random.fold_in(key, 7), (), 0, BLOCKS)
    return counts.at[where].set(SLOTS).astype(jnp.int32)


def draw_tile_rows(key, part):
    subkeys = jax.random.split(jax.random.fold_in(key, 11), BLOCKS)
    chosen = jax.vmap(lambda subkey: jax.random.permutation(subkey, BLOCKS)[:SLOTS])(subkeys)
    return chosen.astype(jnp.int32)


def block_scale(rng, extent, cuts, least, top_value):
    factor_of = 1.0
    for dim, blocks in cuts:
        draws = jax.random.uniform(jax.random.fold_in(jax.random.fold_in(rng, 6), dim), (blocks,), jnp.float32, least / len(cuts), top_value / len(cuts))
        factor_of = factor_of * jnp.repeat(jnp.exp(draws), extent[dim] // blocks).reshape((-1,) + (1,) * (len(extent) - 1 - dim))
    return factor_of


def bell_draw(own_key, shape, spread, most, cuts=(), held_as=jnp.bfloat16):
    values = spread * jax.random.normal(own_key, shape, jnp.float32)
    if cuts:
        values = values * block_scale(own_key, shape, cuts, -0.22, 0.18)
    return jnp.clip(values, -most, most).astype(held_as)


def setup_inputs(seed: int = 0, part: int = 0) -> dict:
    arg_keys = jax.random.split(jax.random.key(seed), 13)
    part_splits = jax.random.split(jax.random.fold_in(arg_keys[12], part), 13)
    pair_slab = bell_draw(part_splits[0], (K, N, C), 1.0, 6.0, ((0, 4), (1, 4)))
    tile_pair = bell_draw(part_splits[1], (BLOCKS, SLOTS, TILE, TILE, C), 1.0, 6.0, ((0, 4), (2, 4)))
    tile_cotan = bell_draw(part_splits[2], (BLOCKS, SLOTS, TILE, TILE, C), 1.0, 6.0, ((0, 4), (2, 4)))
    tile_rows = draw_tile_rows(jax.random.fold_in(jax.random.fold_in(arg_keys[12], part), 71), part)
    tile_count = draw_tile_count(jax.random.fold_in(jax.random.fold_in(arg_keys[12], part), 71), part)
    norm_gain = jnp.clip(1.0 + 0.1 * jax.random.normal(arg_keys[5], (C,), jnp.float32), 0.5, 1.5)
    norm_bias = bell_draw(arg_keys[6], (C,), 0.5, 2.5, (), jnp.float32)
    w_in = bell_draw(arg_keys[7], (C, 4 * H), C ** -0.5, 0.5)
    out_gain = jnp.clip(1.0 + 0.1 * jax.random.normal(arg_keys[8], (H,), jnp.float32), 0.5, 1.5)
    out_bias = bell_draw(arg_keys[9], (H,), 0.5, 2.5, (), jnp.float32)
    w_out = bell_draw(arg_keys[10], (H, C), H ** -0.5, 0.5)
    w_gate = bell_draw(arg_keys[11], (C, C), C ** -0.5, 0.5)
    return {"pair_slab": pair_slab, "tile_pair": tile_pair, "tile_cotan": tile_cotan, "tile_rows": tile_rows, "tile_count": tile_count, "norm_gain": norm_gain, "norm_bias": norm_bias, "w_in": w_in, "out_gain": out_gain, "out_bias": out_bias, "w_out": w_out, "w_gate": w_gate}


epsilon = 1e-05

def normalize(values):
    center = values - lax.optimization_barrier(jnp.mean(values, axis=-1, keepdims=True))
    variance = lax.optimization_barrier(jnp.mean(center * center, axis=-1, keepdims=True))
    inverse = lax.rsqrt(variance + epsilon)
    return (center * inverse, inverse)

def norm_back(grad_in, centred, inverse, gain):
    scaled = grad_in * gain
    first = lax.optimization_barrier(jnp.mean(scaled, axis=-1, keepdims=True))
    second = lax.optimization_barrier(jnp.mean(scaled * centred, axis=-1, keepdims=True))
    return inverse * (scaled - first - centred * second)

def rounded(values):
    return lax.optimization_barrier(values.astype(jnp.bfloat16)).astype(jnp.float32)

def reference(pair_slab, tile_pair, tile_cotan, tile_rows, tile_count, norm_gain, norm_bias, w_in, out_gain, out_bias, w_out, w_gate):
    slab_hat, slab_inv = normalize(pair_slab.astype(jnp.float32))
    slab_norm = (slab_hat * norm_gain + norm_bias).astype(jnp.bfloat16)
    flat_norm = slab_norm.reshape(-1, C)
    project = jnp.dot(flat_norm, w_in, preferred_element_type=jnp.float32).reshape(K, N, 4 * H)
    left_proj = project[..., :H]
    left_sig = jax.nn.sigmoid(project[..., H:2 * H])
    right_proj = project[..., 2 * H:3 * H]
    right_sig = jax.nn.sigmoid(project[..., 3 * H:])
    left_edges = (left_sig * left_proj).astype(jnp.bfloat16)
    right_edges = (right_sig * right_proj).astype(jnp.bfloat16)
    row_part = TILE // N_ROW
    zero_index = jnp.int32(0)

    def one_tile(carry, index):
        left_grad, right_grad, grad_out_w, grad_gate_w = carry
        column = index // SLOTS
        slot = index % SLOTS
        row_block = tile_rows[column, slot]
        active = (slot < tile_count[column]).astype(jnp.float32)
        left_start = (zero_index, (row_block * TILE).astype(jnp.int32), zero_index)
        right_start = (zero_index, (column * TILE).astype(jnp.int32), zero_index)
        left_tile = lax.dynamic_slice(left_edges, left_start, (K, TILE, H)).astype(jnp.float32)
        right_tile = lax.dynamic_slice(right_edges, right_start, (K, TILE, H)).astype(jnp.float32)
        grouped = jnp.einsum('gkih,gkjh->gijh', left_tile.reshape(N_ROW, K_DEV, TILE, H), right_tile.reshape(N_ROW, K_DEV, TILE, H))
        combined = lax.optimization_barrier(jnp.sum(rounded(grouped), axis=0))
        comb_hat, comb_inv = normalize(combined)
        comb_norm = (comb_hat * out_gain + out_bias).astype(jnp.bfloat16)
        pair_hat, pair_inv = normalize(tile_pair[column, slot].astype(jnp.float32))
        pair_norm = (pair_hat * norm_gain + norm_bias).astype(jnp.bfloat16)
        flat_comb = comb_norm.reshape(-1, H)
        flat_pair = pair_norm.reshape(-1, C)
        mixed = jnp.dot(flat_comb, w_out, preferred_element_type=jnp.float32)
        gate = jax.nn.sigmoid(jnp.dot(flat_pair, w_gate, preferred_element_type=jnp.float32))
        update = (active * gate * mixed).astype(jnp.bfloat16)
        cotan = tile_cotan[column, slot].astype(jnp.float32).reshape(-1, C) * active
        grad_mixed = (cotan * gate).astype(jnp.bfloat16)
        grad_logit = (cotan * mixed * gate * (1.0 - gate)).astype(jnp.bfloat16)
        grad_out_w = grad_out_w + jnp.dot(flat_comb.T, grad_mixed, preferred_element_type=jnp.float32)
        grad_gate_w = grad_gate_w + jnp.dot(flat_pair.T, grad_logit, preferred_element_type=jnp.float32)
        grad_comb = jnp.dot(grad_mixed, w_out.T, preferred_element_type=jnp.float32).reshape(TILE, TILE, H)
        grad_pair = jnp.dot(grad_logit, w_gate.T, preferred_element_type=jnp.float32).reshape(TILE, TILE, C)
        pair_back = norm_back(grad_pair, pair_hat, pair_inv, norm_gain).astype(jnp.bfloat16)
        comb_back = rounded(norm_back(grad_comb, comb_hat, comb_inv, out_gain))
        left_term = rounded(jnp.einsum('ijh,kjh->kih', comb_back, right_tile))
        right_groups = jnp.einsum('gijh,kgih->gkjh', comb_back.reshape(N_ROW, row_part, TILE, H), left_tile.reshape(K, N_ROW, row_part, H))
        right_term = lax.optimization_barrier(jnp.sum(rounded(right_groups), axis=0))
        left_old = lax.dynamic_slice(left_grad, left_start, (K, TILE, H))
        left_grad = lax.dynamic_update_slice(left_grad, left_old + left_term, left_start)
        right_old = lax.dynamic_slice(right_grad, right_start, (K, TILE, H))
        right_grad = lax.dynamic_update_slice(right_grad, right_old + right_term, right_start)
        return ((left_grad, right_grad, grad_out_w, grad_gate_w), (update.reshape(TILE, TILE, C), pair_back))
    start = (jnp.zeros((K, N, H), jnp.float32), jnp.zeros((K, N, H), jnp.float32), jnp.zeros((H, C), jnp.float32), jnp.zeros((C, C), jnp.float32))
    carry, stacked = lax.scan(one_tile, start, jnp.arange(BLOCKS * SLOTS, dtype=jnp.int32))
    left_grad, right_grad, grad_out_w, grad_gate_w = carry
    updates = stacked[0].reshape(BLOCKS, SLOTS, TILE, TILE, C)
    grad_tiles = stacked[1].reshape(BLOCKS, SLOTS, TILE, TILE, C)
    left_raw = left_proj
    right_raw = right_proj
    grad_project = jnp.concatenate([left_grad * left_sig, left_grad * left_raw * left_sig * (1.0 - left_sig), right_grad * right_sig, right_grad * right_raw * right_sig * (1.0 - right_sig)], axis=-1).astype(jnp.bfloat16)
    flat_grad = grad_project.reshape(-1, 4 * H)
    grad_in_w = jnp.dot(flat_norm.T, flat_grad, preferred_element_type=jnp.float32)
    grad_norm = jnp.dot(flat_grad, w_in.T, preferred_element_type=jnp.float32).reshape(K, N, C)
    grad_slab = norm_back(grad_norm, slab_hat, slab_inv, norm_gain).astype(jnp.bfloat16)
    return (updates, grad_slab, grad_tiles, grad_in_w, grad_out_w, grad_gate_w)
```

```python
import functools

import jax
import jax.numpy as jnp
from jax import lax
from jax.experimental import pallas as pl
from jax.experimental.pallas import tpu as pltpu
from jax.sharding import PartitionSpec as P

epsilon = 1e-05


def normalize(values):
    center = values - jnp.mean(values, axis=-1, keepdims=True)
    variance = jnp.mean(center * center, axis=-1, keepdims=True)
    inverse = lax.rsqrt(variance + epsilon)
    return (center * inverse, inverse)


def norm_back(grad_in, centred, inverse, gain):
    scaled = grad_in * gain
    first = jnp.mean(scaled, axis=-1, keepdims=True)
    second = jnp.mean(scaled * centred, axis=-1, keepdims=True)
    return inverse * (scaled - first - centred * second)


def dot(left, right, left_dim, right_dim):
    return lax.dot_general(
        left,
        right,
        (((left_dim,), (right_dim,)), ((), ())),
        preferred_element_type=jnp.float32,
    )


def to_hidden_major(values):
    return jnp.swapaxes(jnp.swapaxes(values, 1, 2), 0, 1)


def from_hidden_major(values):
    return jnp.swapaxes(jnp.swapaxes(values, 0, 1), 1, 2)


def tile_kernel(
    rows_ref,
    count_ref,
    panels_ref,
    right_ref,
    pair_ref,
    cotan_ref,
    norm_gain_ref,
    norm_bias_ref,
    out_gain_ref,
    out_bias_ref,
    w_out_ref,
    w_gate_ref,
    update_ref,
    tiles_ref,
    left_ref,
    right_part_ref,
    out_w_ref,
    gate_w_ref,
    left_major,
    right_major,
    comb_major,
    back_major,
    right_back,
    left_back,
):
    depth, tile_len, hidden = right_ref.shape
    slots, row_part, _, channels = pair_ref.shape
    chunk = 16
    norm_gain, norm_bias = norm_gain_ref[...], norm_bias_ref[...]
    out_gain, out_bias = out_gain_ref[...], out_bias_ref[...]

    @pl.loop(0, depth // chunk)
    def _(step):
        at = pl.ds(pl.multiple_of(step * chunk, chunk), chunk)
        block = right_ref[at].astype(jnp.float32)
        right_major[:, at, :] = to_hidden_major(block).astype(jnp.bfloat16)
        parts = [panels_ref[rows_ref[0, s], at] for s in range(slots)]
        block = jnp.concatenate(parts, axis=1).astype(jnp.float32)
        left_major[:, at, :] = to_hidden_major(block).astype(jnp.bfloat16)
        for column in range(left_ref.shape[0]):
            left_ref[column, at] = jnp.zeros((chunk,) + left_ref.shape[2:], left_ref.dtype)

    @pl.loop(0, hidden, unroll=4)
    def _(h):
        comb_major[h] = dot(left_major[h], right_major[h], 0, 0)

    out_w_ref[...] = jnp.zeros_like(out_w_ref)
    gate_w_ref[...] = jnp.zeros_like(gate_w_ref)
    for s in range(slots):
        active = jnp.where(s < count_ref[0], 1.0, 0.0).astype(jnp.float32)

        @pl.loop(0, row_part // chunk)
        def _(step):
            at = pl.ds(pl.multiple_of(step * chunk, chunk), chunk)
            at_all = pl.ds(pl.multiple_of(s * row_part + step * chunk, chunk), chunk)
            combined = from_hidden_major(comb_major[:, at_all, :]).reshape(-1, hidden)
            comb_hat, comb_inv = normalize(combined)
            comb_norm = (comb_hat * out_gain + out_bias).astype(jnp.bfloat16)
            pair = pair_ref[s, at].astype(jnp.float32).reshape(-1, channels)
            pair_hat, pair_inv = normalize(pair)
            pair_norm = (pair_hat * norm_gain + norm_bias).astype(jnp.bfloat16)
            mixed = dot(comb_norm, w_out_ref[...], 1, 0)
            gate = jax.nn.sigmoid(dot(pair_norm, w_gate_ref[...], 1, 0))
            update = (active * gate * mixed).astype(jnp.bfloat16)
            update_ref[s, at] = update.reshape(chunk, tile_len, channels)
            cotan = cotan_ref[s, at].astype(jnp.float32).reshape(-1, channels) * active
            grad_mixed = (cotan * gate).astype(jnp.bfloat16)
            grad_logit = (cotan * mixed * gate * (1.0 - gate)).astype(jnp.bfloat16)
            out_w_ref[...] += dot(comb_norm, grad_mixed, 0, 0)
            gate_w_ref[...] += dot(pair_norm, grad_logit, 0, 0)
            grad_pair = dot(grad_logit, w_gate_ref[...], 1, 1)
            pair_back = norm_back(grad_pair, pair_hat, pair_inv, norm_gain)
            tiles_ref[s, at] = pair_back.astype(jnp.bfloat16).reshape(chunk, tile_len, channels)
            grad_comb = dot(grad_mixed, w_out_ref[...], 1, 1)
            comb_back = norm_back(grad_comb, comb_hat, comb_inv, out_gain)
            comb_back = comb_back.reshape(chunk, tile_len, hidden)
            back_major[:, at_all, :] = to_hidden_major(comb_back).astype(jnp.bfloat16)

    @pl.loop(0, hidden, unroll=4)
    def _(h):
        back = back_major[h]
        right_back[h] = dot(left_major[h], back, 1, 0).astype(jnp.bfloat16)
        left_back[h] = dot(right_major[h], back, 1, 1).astype(jnp.bfloat16)

    @pl.loop(0, depth // chunk)
    def _(step):
        at = pl.ds(pl.multiple_of(step * chunk, chunk), chunk)
        right_part_ref[at] = from_hidden_major(
            right_back[:, at, :].astype(jnp.float32)
        ).astype(jnp.bfloat16)
        terms = from_hidden_major(left_back[:, at, :].astype(jnp.float32)).astype(jnp.bfloat16)
        for s in range(slots):
            row = rows_ref[0, s]
            left_ref[row, at] += terms[:, s * row_part : (s + 1) * row_part]


def tile_work(rows, count, panels, right_full, pair, cotan, gains, w_out, w_gate):
    depth, tile_len, hidden = right_full.shape
    slots, row_part, _, channels = pair.shape
    cells = slots * row_part
    smem = pl.BlockSpec(memory_space=pltpu.SMEM)
    vmem = pl.BlockSpec(memory_space=pltpu.VMEM)
    half, full = jnp.bfloat16, jnp.float32
    return pl.pallas_call(
        tile_kernel,
        out_shape=(
            jax.ShapeDtypeStruct(pair.shape, half),
            jax.ShapeDtypeStruct(pair.shape, half),
            jax.ShapeDtypeStruct(panels.shape, half),
            jax.ShapeDtypeStruct(right_full.shape, half),
            jax.ShapeDtypeStruct((hidden, channels), full),
            jax.ShapeDtypeStruct((channels, channels), full),
        ),
        in_specs=[smem, smem] + [vmem] * 10,
        out_specs=(vmem,) * 6,
        scratch_shapes=[
            pltpu.VMEM((hidden, depth, cells), half),
            pltpu.VMEM((hidden, depth, tile_len), half),
            pltpu.VMEM((hidden, cells, tile_len), full),
            pltpu.VMEM((hidden, cells, tile_len), half),
            pltpu.VMEM((hidden, depth, tile_len), half),
            pltpu.VMEM((hidden, depth, cells), half),
        ],
        compiler_params=pltpu.CompilerParams(vmem_limit_bytes=58 * 2**20),
        name="tile_work",
    )(rows, count, panels, right_full, pair, cotan, *gains, w_out, w_gate)


def sum_kernel(col_count, row_count, grads_ref, total_ref, outgoing, arrived, summed, sems):
    count, rows, _ = grads_ref.shape
    group = lax.axis_index("groups")
    me = lax.axis_index("col") * row_count + lax.axis_index("row")

    def place(index):
        return (group, index // row_count, index % row_count)

    def piece(step):
        to = (me + step) % count
        return pltpu.make_async_remote_copy(
            src_ref=outgoing.at[step],
            dst_ref=arrived.at[step],
            send_sem=sems.at[0, step],
            recv_sem=sems.at[1, step],
            device_id=place(to),
            device_id_type=pl.DeviceIdType.MESH,
        )

    def share(step):
        to = (me + step) % count
        return pltpu.make_async_remote_copy(
            src_ref=summed.at[0],
            dst_ref=summed.at[step],
            send_sem=sems.at[2, step],
            recv_sem=sems.at[3, step],
            device_id=place(to),
            device_id_type=pl.DeviceIdType.MESH,
        )

    barrier = pltpu.get_barrier_semaphore()

    @pl.loop(1, count)
    def _(step):
        pl.semaphore_signal(
            barrier,
            inc=1,
            device_id=place((me + step) % count),
            device_id_type=pl.DeviceIdType.MESH,
        )

    @pl.loop(1, count)
    def _(step):
        outgoing[step] = grads_ref[(me + step) % count].astype(jnp.bfloat16)

    pl.semaphore_wait(barrier, count - 1)

    @pl.loop(1, count)
    def _(step):
        piece(step).start()

    @pl.loop(1, count)
    def _(step):
        piece(step).wait()

    total = grads_ref[me]
    for step in range(1, count):
        total = total + arrived[step].astype(jnp.float32)
    summed[0] = total.astype(jnp.bfloat16)

    @pl.loop(1, count)
    def _(step):
        share(step).start()

    @pl.loop(1, count)
    def _(step):
        share(step).wait()

    @pl.loop(0, count)
    def _(step):
        total_ref[(me + count - step) % count] = summed[step].astype(jnp.float32)


def sum_over_devices(grads, col_count, row_count):
    count, rows, lanes = grads.shape
    vmem = pl.BlockSpec(memory_space=pltpu.VMEM)
    return pl.pallas_call(
        functools.partial(sum_kernel, col_count, row_count),
        out_shape=jax.ShapeDtypeStruct(grads.shape, grads.dtype),
        in_specs=[vmem],
        out_specs=vmem,
        scratch_shapes=[
            pltpu.VMEM((count, rows, lanes), jnp.bfloat16),
            pltpu.VMEM((count, rows, lanes), jnp.bfloat16),
            pltpu.VMEM((count, rows, lanes), jnp.bfloat16),
            pltpu.SemaphoreType.DMA((4, count)),
        ],
        compiler_params=pltpu.CompilerParams(collective_id=0, has_side_effects=True),
        name="sum_over_devices",
    )(grads)


def body(
    pair_slab,
    tile_pair,
    tile_cotan,
    tile_rows,
    tile_count,
    norm_gain,
    norm_bias,
    w_in,
    out_gain,
    out_bias,
    w_out,
    w_gate,
):
    k_local, tile_len, channels = pair_slab.shape
    hidden_w = w_out.shape[0]
    slots = tile_rows.shape[1]
    row_count = lax.axis_size("row")
    col_count = lax.axis_size("col")
    row_part = tile_len // row_count
    slab_hat, slab_inv = normalize(pair_slab.astype(jnp.float32))
    slab_norm = (slab_hat * norm_gain + norm_bias).astype(jnp.bfloat16)
    flat_norm = slab_norm.reshape(-1, channels)
    project = jnp.dot(flat_norm, w_in, preferred_element_type=jnp.float32).reshape(
        k_local, tile_len, 4 * hidden_w
    )
    left_proj = project[..., :hidden_w]
    left_sig = jax.nn.sigmoid(project[..., hidden_w : 2 * hidden_w])
    right_proj = project[..., 2 * hidden_w : 3 * hidden_w]
    right_sig = jax.nn.sigmoid(project[..., 3 * hidden_w :])
    left_edges = (left_sig * left_proj).astype(jnp.bfloat16)
    right_edges = (right_sig * right_proj).astype(jnp.bfloat16)
    spread = lax.all_to_all(
        left_edges.reshape(k_local, row_count, row_part, hidden_w),
        "row",
        split_axis=1,
        concat_axis=0,
        tiled=True,
    )
    panels = lax.all_gather(spread, "col")
    right_full = lax.all_gather(right_edges, "row", axis=0, tiled=True)
    update, pair_back, routed, right_part, out_total, gate_total = tile_work(
        tile_rows,
        tile_count,
        panels.reshape(col_count, -1, row_part, hidden_w),
        right_full,
        tile_pair[0],
        tile_cotan[0],
        tuple(v[None, :] for v in (norm_gain, norm_bias, out_gain, out_bias)),
        w_out,
        w_gate,
    )
    column_sum = lax.psum_scatter(
        routed, "col", scatter_dimension=0, tiled=True
    ).astype(jnp.float32)
    returned = lax.all_to_all(
        column_sum.reshape(row_count, k_local, row_part, hidden_w).astype(jnp.bfloat16),
        "row",
        split_axis=0,
        concat_axis=2,
        tiled=True,
    ).astype(jnp.float32)
    left_grad = returned.reshape(k_local, tile_len, hidden_w)
    right_grad = lax.psum_scatter(
        right_part, "row", scatter_dimension=0, tiled=True
    ).astype(jnp.float32)
    grad_project = jnp.concatenate(
        [
            left_grad * left_sig,
            left_grad * left_proj * left_sig * (1.0 - left_sig),
            right_grad * right_sig,
            right_grad * right_proj * right_sig * (1.0 - right_sig),
        ],
        axis=-1,
    ).astype(jnp.bfloat16)
    flat_grad = grad_project.reshape(-1, 4 * hidden_w)
    grad_in_w = jnp.dot(flat_norm.T, flat_grad, preferred_element_type=jnp.float32)
    grad_norm = jnp.dot(flat_grad, w_in.T, preferred_element_type=jnp.float32).reshape(
        k_local, tile_len, channels
    )
    grad_slab = norm_back(grad_norm, slab_hat, slab_inv, norm_gain).astype(jnp.bfloat16)
    devices = row_count * col_count
    lanes = 128
    grads = [v.reshape(-1, lanes) for v in (grad_in_w, out_total, gate_total)]
    sizes = [v.shape[0] for v in grads]
    rows = -(-sum(sizes) // (16 * devices)) * 16
    spare = rows * devices - sum(sizes)
    grads = jnp.concatenate(grads + [jnp.zeros((spare, lanes), jnp.float32)] * (spare > 0))
    summed = sum_over_devices(grads.reshape(devices, rows, lanes), col_count, row_count)
    summed = summed.reshape(-1, lanes)
    in_total = summed[: sizes[0]].reshape(grad_in_w.shape)
    out_total = summed[sizes[0] : sizes[0] + sizes[1]].reshape(out_total.shape)
    gate_total = summed[sizes[0] + sizes[1] : sum(sizes)].reshape(gate_total.shape)
    update_out = update.reshape(1, slots, row_part, tile_len, channels)
    tiles_out = pair_back.reshape(1, slots, row_part, tile_len, channels)
    return (update_out, grad_slab, tiles_out, in_total, out_total, gate_total)


def solution(mesh):
    return jax.shard_map(
        body,
        mesh=mesh,
        in_specs=(
            P(("groups", "row"), "col", None),
            P(("groups", "col"), None, "row", None, None),
            P(("groups", "col"), None, "row", None, None),
            P(("groups", "col"), None),
            P(("groups", "col")),
            P(),
            P(),
            P(),
            P(),
            P(),
            P(),
            P(),
        ),
        out_specs=(
            P(("groups", "col"), None, "row", None, None),
            P(("groups", "row"), "col", None),
            P(("groups", "col"), None, "row", None, None),
            P("groups", None),
            P("groups", None),
            P("groups", None),
        ),
        check_vma=False,
    )
```

```python
import functools

import jax
import jax.numpy as jnp
from jax import lax
from jax.experimental import pallas as pl
from jax.experimental.pallas import tpu as pltpu
from jax.sharding import PartitionSpec as P

epsilon = 1e-05


def normalize(values):
    center = values - jnp.mean(values, axis=-1, keepdims=True)
    variance = jnp.mean(center * center, axis=-1, keepdims=True)
    inverse = lax.rsqrt(variance + epsilon)
    return (center * inverse, inverse)


def norm_back(grad_in, centred, inverse, gain):
    scaled = grad_in * gain
    first = jnp.mean(scaled, axis=-1, keepdims=True)
    second = jnp.mean(scaled * centred, axis=-1, keepdims=True)
    return inverse * (scaled - first - centred * second)


def dot(left, right, left_dim, right_dim):
    return lax.dot_general(
        left,
        right,
        (((left_dim,), (right_dim,)), ((), ())),
        preferred_element_type=jnp.float32,
    )


def to_hidden_major(values):
    return jnp.swapaxes(jnp.swapaxes(values, 1, 2), 0, 1)


def from_hidden_major(values):
    return jnp.swapaxes(jnp.swapaxes(values, 0, 1), 1, 2)


def tile_kernel(
    rows_ref,
    count_ref,
    panels_ref,
    right_ref,
    pair_ref,
    cotan_ref,
    norm_gain_ref,
    norm_bias_ref,
    out_gain_ref,
    out_bias_ref,
    w_out_ref,
    w_gate_ref,
    update_ref,
    tiles_ref,
    left_ref,
    right_part_ref,
    out_w_ref,
    gate_w_ref,
    left_major,
    right_major,
    comb_major,
    back_major,
    right_back,
    left_back,
):
    depth, tile_len, hidden = right_ref.shape
    slots, row_part, _, channels = pair_ref.shape
    chunk = 16
    norm_gain, norm_bias = norm_gain_ref[...], norm_bias_ref[...]
    out_gain, out_bias = out_gain_ref[...], out_bias_ref[...]

    @pl.loop(0, depth // chunk)
    def _(step):
        at = pl.ds(pl.multiple_of(step * chunk, chunk), chunk)
        block = right_ref[at].astype(jnp.float32)
        right_major[:, at, :] = to_hidden_major(block).astype(jnp.bfloat16)
        parts = [panels_ref[rows_ref[0, s], at] for s in range(slots)]
        block = jnp.concatenate(parts, axis=1).astype(jnp.float32)
        left_major[:, at, :] = to_hidden_major(block).astype(jnp.bfloat16)
        for column in range(left_ref.shape[0]):
            left_ref[column, at] = jnp.zeros((chunk,) + left_ref.shape[2:], left_ref.dtype)

    @pl.loop(0, hidden, unroll=4)
    def _(h):
        comb_major[h] = dot(left_major[h], right_major[h], 0, 0)

    out_w_ref[...] = jnp.zeros_like(out_w_ref)
    gate_w_ref[...] = jnp.zeros_like(gate_w_ref)
    for s in range(slots):
        active = jnp.where(s < count_ref[0], 1.0, 0.0).astype(jnp.float32)

        @pl.loop(0, row_part // chunk)
        def _(step):
            at = pl.ds(pl.multiple_of(step * chunk, chunk), chunk)
            at_all = pl.ds(pl.multiple_of(s * row_part + step * chunk, chunk), chunk)
            combined = from_hidden_major(comb_major[:, at_all, :]).reshape(-1, hidden)
            comb_hat, comb_inv = normalize(combined)
            comb_norm = (comb_hat * out_gain + out_bias).astype(jnp.bfloat16)
            pair = pair_ref[s, at].astype(jnp.float32).reshape(-1, channels)
            pair_hat, pair_inv = normalize(pair)
            pair_norm = (pair_hat * norm_gain + norm_bias).astype(jnp.bfloat16)
            mixed = dot(comb_norm, w_out_ref[...], 1, 0)
            gate = jax.nn.sigmoid(dot(pair_norm, w_gate_ref[...], 1, 0))
            update = (active * gate * mixed).astype(jnp.bfloat16)
            update_ref[s, at] = update.reshape(chunk, tile_len, channels)
            cotan = cotan_ref[s, at].astype(jnp.float32).reshape(-1, channels) * active
            grad_mixed = (cotan * gate).astype(jnp.bfloat16)
            grad_logit = (cotan * mixed * gate * (1.0 - gate)).astype(jnp.bfloat16)
            out_w_ref[...] += dot(comb_norm, grad_mixed, 0, 0)
            gate_w_ref[...] += dot(pair_norm, grad_logit, 0, 0)
            grad_pair = dot(grad_logit, w_gate_ref[...], 1, 1)
            pair_back = norm_back(grad_pair, pair_hat, pair_inv, norm_gain)
            tiles_ref[s, at] = pair_back.astype(jnp.bfloat16).reshape(chunk, tile_len, channels)
            grad_comb = dot(grad_mixed, w_out_ref[...], 1, 1)
            comb_back = norm_back(grad_comb, comb_hat, comb_inv, out_gain)
            comb_back = comb_back.reshape(chunk, tile_len, hidden)
            back_major[:, at_all, :] = to_hidden_major(comb_back).astype(jnp.bfloat16)

    @pl.loop(0, hidden, unroll=4)
    def _(h):
        back = back_major[h]
        right_back[h] = dot(left_major[h], back, 1, 0).astype(jnp.bfloat16)
        left_back[h] = dot(right_major[h], back, 1, 1).astype(jnp.bfloat16)

    @pl.loop(0, depth // chunk)
    def _(step):
        at = pl.ds(pl.multiple_of(step * chunk, chunk), chunk)
        right_part_ref[at] = from_hidden_major(
            right_back[:, at, :].astype(jnp.float32)
        ).astype(jnp.bfloat16)
        terms = from_hidden_major(left_back[:, at, :].astype(jnp.float32)).astype(jnp.bfloat16)
        for s in range(slots):
            row = rows_ref[0, s]
            left_ref[row, at] += terms[:, s * row_part : (s + 1) * row_part]


def tile_work(rows, count, panels, right_full, pair, cotan, gains, w_out, w_gate):
    depth, tile_len, hidden = right_full.shape
    slots, row_part, _, channels = pair.shape
    cells = slots * row_part
    smem = pl.BlockSpec(memory_space=pltpu.SMEM)
    vmem = pl.BlockSpec(memory_space=pltpu.VMEM)
    half, full = jnp.bfloat16, jnp.float32
    return pl.pallas_call(
        tile_kernel,
        out_shape=(
            jax.ShapeDtypeStruct(pair.shape, half),
            jax.ShapeDtypeStruct(pair.shape, half),
            jax.ShapeDtypeStruct(panels.shape, half),
            jax.ShapeDtypeStruct(right_full.shape, half),
            jax.ShapeDtypeStruct((hidden, channels), full),
            jax.ShapeDtypeStruct((channels, channels), full),
        ),
        in_specs=[smem, smem] + [vmem] * 10,
        out_specs=(vmem,) * 6,
        scratch_shapes=[
            pltpu.VMEM((hidden, depth, cells), half),
            pltpu.VMEM((hidden, depth, tile_len), half),
            pltpu.VMEM((hidden, cells, tile_len), full),
            pltpu.VMEM((hidden, cells, tile_len), half),
            pltpu.VMEM((hidden, depth, tile_len), half),
            pltpu.VMEM((hidden, depth, cells), half),
        ],
        compiler_params=pltpu.CompilerParams(vmem_limit_bytes=58 * 2**20),
        name="tile_work",
    )(rows, count, panels, right_full, pair, cotan, *gains, w_out, w_gate)


def sum_kernel(col_count, row_count, grads_ref, total_ref, outgoing, arrived, summed, sems):
    count, rows, _ = grads_ref.shape
    group = lax.axis_index("groups")
    me = lax.axis_index("col") * row_count + lax.axis_index("row")

    def place(index):
        return (group, index // row_count, index % row_count)

    def piece(step):
        to = (me + step) % count
        return pltpu.make_async_remote_copy(
            src_ref=outgoing.at[step],
            dst_ref=arrived.at[step],
            send_sem=sems.at[0, step],
            recv_sem=sems.at[1, step],
            device_id=place(to),
            device_id_type=pl.DeviceIdType.MESH,
        )

    def share(step):
        to = (me + step) % count
        return pltpu.make_async_remote_copy(
            src_ref=summed.at[0],
            dst_ref=summed.at[step],
            send_sem=sems.at[2, step],
            recv_sem=sems.at[3, step],
            device_id=place(to),
            device_id_type=pl.DeviceIdType.MESH,
        )

    barrier = pltpu.get_barrier_semaphore()

    @pl.loop(1, count)
    def _(step):
        pl.semaphore_signal(
            barrier,
            inc=1,
            device_id=place((me + step) % count),
            device_id_type=pl.DeviceIdType.MESH,
        )

    @pl.loop(1, count)
    def _(step):
        outgoing[step] = grads_ref[(me + step) % count].astype(jnp.bfloat16)

    pl.semaphore_wait(barrier, count - 1)

    @pl.loop(1, count)
    def _(step):
        piece(step).start()

    @pl.loop(1, count)
    def _(step):
        piece(step).wait()

    total = grads_ref[me]
    for step in range(1, count):
        total = total + arrived[step].astype(jnp.float32)
    summed[0] = total.astype(jnp.bfloat16)

    @pl.loop(1, count)
    def _(step):
        share(step).start()

    @pl.loop(1, count)
    def _(step):
        share(step).wait()

    @pl.loop(0, count)
    def _(step):
        total_ref[(me + count - step) % count] = summed[step].astype(jnp.float32)


def sum_over_devices(grads, col_count, row_count):
    count, rows, lanes = grads.shape
    vmem = pl.BlockSpec(memory_space=pltpu.VMEM)
    return pl.pallas_call(
        functools.partial(sum_kernel, col_count, row_count),
        out_shape=jax.ShapeDtypeStruct(grads.shape, grads.dtype),
        in_specs=[vmem],
        out_specs=vmem,
        scratch_shapes=[
            pltpu.VMEM((count, rows, lanes), jnp.bfloat16),
            pltpu.VMEM((count, rows, lanes), jnp.bfloat16),
            pltpu.VMEM((count, rows, lanes), jnp.bfloat16),
            pltpu.SemaphoreType.DMA((4, count)),
        ],
        compiler_params=pltpu.CompilerParams(collective_id=0, has_side_effects=True),
        name="sum_over_devices",
    )(grads)


def exchange_kernel(
    forward,
    col_count,
    row_count,
    left_ref,
    right_ref,
    left_out,
    right_out,
    left_sems,
    right_sems,
):
    group, col, row = lax.axis_index("groups"), lax.axis_index("col"), lax.axis_index("row")
    count = col_count * row_count
    me = col * row_count + row
    if forward:
        depth, part = left_ref.shape[0], left_ref.shape[1] // row_count
    else:
        depth, part = left_ref.shape[1] // row_count, left_ref.shape[2]

    def slab(index):
        return pl.ds(pl.multiple_of(index * depth, depth), depth)

    def cells(index):
        return pl.ds(pl.multiple_of(index * part, part), part)

    def left_ends(to_col, to_row):
        if forward:
            return left_ref.at[:, cells(to_row)], left_out.at[col, slab(row)]
        return left_ref.at[to_col, slab(to_row)], left_out.at[col, :, cells(row)]

    def right_ends(to_row):
        if forward:
            return right_ref, right_out.at[slab(row)]
        return right_ref.at[slab(to_row)], right_out.at[row]

    def send(ends, sems, step, to_col, to_row):
        return pltpu.make_async_remote_copy(
            src_ref=ends[0],
            dst_ref=ends[1],
            send_sem=sems.at[0, step],
            recv_sem=sems.at[1, step],
            device_id=(group, to_col, to_row),
            device_id_type=pl.DeviceIdType.MESH,
        )

    def left_copy(step):
        to = (me + step) % count
        to_col, to_row = to // row_count, to % row_count
        return send(left_ends(to_col, to_row), left_sems, step, to_col, to_row)

    def right_copy(step):
        to_row = (row + step) % row_count
        return send(right_ends(to_row), right_sems, step, col, to_row)

    barrier = pltpu.get_barrier_semaphore()

    @pl.loop(1, count)
    def _(step):
        to = (me + step) % count
        pl.semaphore_signal(
            barrier,
            inc=1,
            device_id=(group, to // row_count, to % row_count),
            device_id_type=pl.DeviceIdType.MESH,
        )

    own_left = pltpu.make_async_copy(*left_ends(col, row), left_sems.at[0, 0])
    own_right = pltpu.make_async_copy(*right_ends(row), right_sems.at[0, 0])
    own_left.start()
    own_right.start()
    pl.semaphore_wait(barrier, count - 1)

    @pl.loop(1, count)
    def _(step):
        left_copy(step).start()

    @pl.loop(1, row_count)
    def _(step):
        right_copy(step).start()

    own_left.wait()
    own_right.wait()

    @pl.loop(1, count)
    def _(step):
        left_copy(step).wait()

    @pl.loop(1, row_count)
    def _(step):
        right_copy(step).wait()


def exchange(forward, left, right, left_shape, right_shape, col_count, row_count):
    anywhere = pl.BlockSpec(memory_space=pl.ANY)
    return pl.pallas_call(
        functools.partial(exchange_kernel, forward, col_count, row_count),
        out_shape=(
            jax.ShapeDtypeStruct(left_shape, left.dtype),
            jax.ShapeDtypeStruct(right_shape, right.dtype),
        ),
        in_specs=[anywhere, anywhere],
        out_specs=(anywhere, anywhere),
        scratch_shapes=[
            pltpu.SemaphoreType.DMA((2, col_count * row_count)),
            pltpu.SemaphoreType.DMA((2, row_count)),
        ],
        compiler_params=pltpu.CompilerParams(
            collective_id=1 if forward else 2, has_side_effects=True
        ),
        name="gather_edges" if forward else "scatter_terms",
    )(left, right)


def body(
    pair_slab,
    tile_pair,
    tile_cotan,
    tile_rows,
    tile_count,
    norm_gain,
    norm_bias,
    w_in,
    out_gain,
    out_bias,
    w_out,
    w_gate,
):
    k_local, tile_len, channels = pair_slab.shape
    hidden_w = w_out.shape[0]
    slots = tile_rows.shape[1]
    row_count = lax.axis_size("row")
    col_count = lax.axis_size("col")
    row_part = tile_len // row_count
    slab_hat, slab_inv = normalize(pair_slab.astype(jnp.float32))
    slab_norm = (slab_hat * norm_gain + norm_bias).astype(jnp.bfloat16)
    flat_norm = slab_norm.reshape(-1, channels)
    project = jnp.dot(flat_norm, w_in, preferred_element_type=jnp.float32).reshape(
        k_local, tile_len, 4 * hidden_w
    )
    left_proj = project[..., :hidden_w]
    left_sig = jax.nn.sigmoid(project[..., hidden_w : 2 * hidden_w])
    right_proj = project[..., 2 * hidden_w : 3 * hidden_w]
    right_sig = jax.nn.sigmoid(project[..., 3 * hidden_w :])
    left_edges = (left_sig * left_proj).astype(jnp.bfloat16)
    right_edges = (right_sig * right_proj).astype(jnp.bfloat16)
    depth = k_local * row_count
    panels, right_full = exchange(
        True,
        left_edges,
        right_edges,
        (col_count, depth, row_part, hidden_w),
        (depth, tile_len, hidden_w),
        col_count,
        row_count,
    )
    update, pair_back, routed, right_part, out_total, gate_total = tile_work(
        tile_rows,
        tile_count,
        panels,
        right_full,
        tile_pair[0],
        tile_cotan[0],
        tuple(v[None, :] for v in (norm_gain, norm_bias, out_gain, out_bias)),
        w_out,
        w_gate,
    )
    left_terms, right_terms = exchange(
        False,
        routed,
        right_part,
        (col_count, k_local, tile_len, hidden_w),
        (row_count, k_local, tile_len, hidden_w),
        col_count,
        row_count,
    )
    left_grad = jnp.sum(left_terms.astype(jnp.float32), axis=0)
    right_grad = jnp.sum(right_terms.astype(jnp.float32), axis=0)
    grad_project = jnp.concatenate(
        [
            left_grad * left_sig,
            left_grad * left_proj * left_sig * (1.0 - left_sig),
            right_grad * right_sig,
            right_grad * right_proj * right_sig * (1.0 - right_sig),
        ],
        axis=-1,
    ).astype(jnp.bfloat16)
    flat_grad = grad_project.reshape(-1, 4 * hidden_w)
    grad_in_w = jnp.dot(flat_norm.T, flat_grad, preferred_element_type=jnp.float32)
    grad_norm = jnp.dot(flat_grad, w_in.T, preferred_element_type=jnp.float32).reshape(
        k_local, tile_len, channels
    )
    grad_slab = norm_back(grad_norm, slab_hat, slab_inv, norm_gain).astype(jnp.bfloat16)
    devices = row_count * col_count
    lanes = 128
    grads = [v.reshape(-1, lanes) for v in (grad_in_w, out_total, gate_total)]
    sizes = [v.shape[0] for v in grads]
    rows = -(-sum(sizes) // (16 * devices)) * 16
    spare = rows * devices - sum(sizes)
    grads = jnp.concatenate(grads + [jnp.zeros((spare, lanes), jnp.float32)] * (spare > 0))
    summed = sum_over_devices(grads.reshape(devices, rows, lanes), col_count, row_count)
    summed = summed.reshape(-1, lanes)
    in_total = summed[: sizes[0]].reshape(grad_in_w.shape)
    out_total = summed[sizes[0] : sizes[0] + sizes[1]].reshape(out_total.shape)
    gate_total = summed[sizes[0] + sizes[1] : sum(sizes)].reshape(gate_total.shape)
    update_out = update.reshape(1, slots, row_part, tile_len, channels)
    tiles_out = pair_back.reshape(1, slots, row_part, tile_len, channels)
    return (update_out, grad_slab, tiles_out, in_total, out_total, gate_total)


def solution(mesh):
    return jax.shard_map(
        body,
        mesh=mesh,
        in_specs=(
            P(("groups", "row"), "col", None),
            P(("groups", "col"), None, "row", None, None),
            P(("groups", "col"), None, "row", None, None),
            P(("groups", "col"), None),
            P(("groups", "col")),
            P(),
            P(),
            P(),
            P(),
            P(),
            P(),
            P(),
        ),
        out_specs=(
            P(("groups", "col"), None, "row", None, None),
            P(("groups", "row"), "col", None),
            P(("groups", "col"), None, "row", None, None),
            P("groups", None),
            P("groups", None),
            P("groups", None),
        ),
        check_vma=False,
    )
```

```python
import functools

import jax
import jax.numpy as jnp
from jax import lax
from jax.experimental import pallas as pl
from jax.experimental.pallas import tpu as pltpu
from jax.sharding import PartitionSpec as P

epsilon = 1e-05


def normalize(values):
    center = values - jnp.mean(values, axis=-1, keepdims=True)
    variance = jnp.mean(center * center, axis=-1, keepdims=True)
    inverse = lax.rsqrt(variance + epsilon)
    return (center * inverse, inverse)


def norm_back(grad_in, centred, inverse, gain):
    scaled = grad_in * gain
    first = jnp.mean(scaled, axis=-1, keepdims=True)
    second = jnp.mean(scaled * centred, axis=-1, keepdims=True)
    return inverse * (scaled - first - centred * second)


def dot(left, right, left_dim, right_dim):
    return lax.dot_general(
        left,
        right,
        (((left_dim,), (right_dim,)), ((), ())),
        preferred_element_type=jnp.float32,
    )


def to_hidden_major(values):
    return jnp.swapaxes(jnp.swapaxes(values, 1, 2), 0, 1)


def from_hidden_major(values):
    return jnp.swapaxes(jnp.swapaxes(values, 0, 1), 1, 2)


def tile_kernel(
    rows_ref,
    count_ref,
    panels_ref,
    right_ref,
    pair_ref,
    cotan_ref,
    norm_gain_ref,
    norm_bias_ref,
    out_gain_ref,
    out_bias_ref,
    w_out_ref,
    w_gate_ref,
    update_ref,
    tiles_ref,
    left_ref,
    right_part_ref,
    out_w_ref,
    gate_w_ref,
    left_major,
    right_major,
    comb_major,
    back_major,
    right_back,
    left_back,
):
    depth, tile_len, hidden = right_ref.shape
    slots, row_part, _, channels = pair_ref.shape
    chunk = 16
    norm_gain, norm_bias = norm_gain_ref[...], norm_bias_ref[...]
    out_gain, out_bias = out_gain_ref[...], out_bias_ref[...]

    @pl.loop(0, depth // chunk)
    def _(step):
        at = pl.ds(pl.multiple_of(step * chunk, chunk), chunk)
        block = right_ref[at].astype(jnp.float32)
        right_major[:, at, :] = to_hidden_major(block).astype(jnp.bfloat16)
        parts = [panels_ref[rows_ref[0, s], at] for s in range(slots)]
        block = jnp.concatenate(parts, axis=1).astype(jnp.float32)
        left_major[:, at, :] = to_hidden_major(block).astype(jnp.bfloat16)
        for column in range(left_ref.shape[0]):
            left_ref[column, at] = jnp.zeros((chunk,) + left_ref.shape[2:], left_ref.dtype)

    @pl.loop(0, hidden, unroll=16)
    def _(h):
        comb_major[h] = dot(left_major[h], right_major[h], 0, 0)

    out_w_ref[...] = jnp.zeros_like(out_w_ref)
    gate_w_ref[...] = jnp.zeros_like(gate_w_ref)
    for s in range(slots):
        active = jnp.where(s < count_ref[0], 1.0, 0.0).astype(jnp.float32)

        @pl.loop(0, row_part // chunk)
        def _(step):
            at = pl.ds(pl.multiple_of(step * chunk, chunk), chunk)
            at_all = pl.ds(pl.multiple_of(s * row_part + step * chunk, chunk), chunk)
            combined = from_hidden_major(comb_major[:, at_all, :]).reshape(-1, hidden)
            comb_hat, comb_inv = normalize(combined)
            comb_norm = (comb_hat * out_gain + out_bias).astype(jnp.bfloat16)
            pair = pair_ref[s, at].astype(jnp.float32).reshape(-1, channels)
            pair_hat, pair_inv = normalize(pair)
            pair_norm = (pair_hat * norm_gain + norm_bias).astype(jnp.bfloat16)
            mixed = dot(comb_norm, w_out_ref[...], 1, 0)
            gate = jax.nn.sigmoid(dot(pair_norm, w_gate_ref[...], 1, 0))
            update = (active * gate * mixed).astype(jnp.bfloat16)
            update_ref[s, at] = update.reshape(chunk, tile_len, channels)
            cotan = cotan_ref[s, at].astype(jnp.float32).reshape(-1, channels) * active
            grad_mixed = (cotan * gate).astype(jnp.bfloat16)
            grad_logit = (cotan * mixed * gate * (1.0 - gate)).astype(jnp.bfloat16)
            out_w_ref[...] += dot(comb_norm, grad_mixed, 0, 0)
            gate_w_ref[...] += dot(pair_norm, grad_logit, 0, 0)
            grad_pair = dot(grad_logit, w_gate_ref[...], 1, 1)
            pair_back = norm_back(grad_pair, pair_hat, pair_inv, norm_gain)
            tiles_ref[s, at] = pair_back.astype(jnp.bfloat16).reshape(chunk, tile_len, channels)
            grad_comb = dot(grad_mixed, w_out_ref[...], 1, 1)
            comb_back = norm_back(grad_comb, comb_hat, comb_inv, out_gain)
            comb_back = comb_back.reshape(chunk, tile_len, hidden)
            back_major[:, at_all, :] = to_hidden_major(comb_back).astype(jnp.bfloat16)

    @pl.loop(0, hidden, unroll=16)
    def _(h):
        back = back_major[h]
        right_back[h] = dot(left_major[h], back, 1, 0).astype(jnp.bfloat16)
        left_back[h] = dot(right_major[h], back, 1, 1).astype(jnp.bfloat16)

    @pl.loop(0, depth // chunk)
    def _(step):
        at = pl.ds(pl.multiple_of(step * chunk, chunk), chunk)
        right_part_ref[at] = from_hidden_major(
            right_back[:, at, :].astype(jnp.float32)
        ).astype(jnp.bfloat16)
        terms = from_hidden_major(left_back[:, at, :].astype(jnp.float32)).astype(jnp.bfloat16)
        for s in range(slots):
            row = rows_ref[0, s]
            left_ref[row, at] += terms[:, s * row_part : (s + 1) * row_part]


def tile_work(rows, count, panels, right_full, pair, cotan, gains, w_out, w_gate):
    depth, tile_len, hidden = right_full.shape
    slots, row_part, _, channels = pair.shape
    cells = slots * row_part
    smem = pl.BlockSpec(memory_space=pltpu.SMEM)
    vmem = pl.BlockSpec(memory_space=pltpu.VMEM)
    half, full = jnp.bfloat16, jnp.float32
    return pl.pallas_call(
        tile_kernel,
        out_shape=(
            jax.ShapeDtypeStruct(pair.shape, half),
            jax.ShapeDtypeStruct(pair.shape, half),
            jax.ShapeDtypeStruct(panels.shape, half),
            jax.ShapeDtypeStruct(right_full.shape, half),
            jax.ShapeDtypeStruct((hidden, channels), full),
            jax.ShapeDtypeStruct((channels, channels), full),
        ),
        in_specs=[smem, smem] + [vmem] * 10,
        out_specs=(vmem,) * 6,
        scratch_shapes=[
            pltpu.VMEM((hidden, depth, cells), half),
            pltpu.VMEM((hidden, depth, tile_len), half),
            pltpu.VMEM((hidden, cells, tile_len), full),
            pltpu.VMEM((hidden, cells, tile_len), half),
            pltpu.VMEM((hidden, depth, tile_len), half),
            pltpu.VMEM((hidden, depth, cells), half),
        ],
        compiler_params=pltpu.CompilerParams(vmem_limit_bytes=58 * 2**20),
        name="tile_work",
    )(rows, count, panels, right_full, pair, cotan, *gains, w_out, w_gate)


def sum_kernel(col_count, row_count, grads_ref, total_ref, outgoing, arrived, summed, sems):
    count, rows, _ = grads_ref.shape
    group = lax.axis_index("groups")
    me = lax.axis_index("col") * row_count + lax.axis_index("row")

    def place(index):
        return (group, index // row_count, index % row_count)

    def piece(step):
        to = (me + step) % count
        return pltpu.make_async_remote_copy(
            src_ref=outgoing.at[step],
            dst_ref=arrived.at[step],
            send_sem=sems.at[0, step],
            recv_sem=sems.at[1, step],
            device_id=place(to),
            device_id_type=pl.DeviceIdType.MESH,
        )

    def share(step):
        to = (me + step) % count
        return pltpu.make_async_remote_copy(
            src_ref=summed.at[0],
            dst_ref=summed.at[step],
            send_sem=sems.at[2, step],
            recv_sem=sems.at[3, step],
            device_id=place(to),
            device_id_type=pl.DeviceIdType.MESH,
        )

    barrier = pltpu.get_barrier_semaphore()

    @pl.loop(1, count)
    def _(step):
        pl.semaphore_signal(
            barrier,
            inc=1,
            device_id=place((me + step) % count),
            device_id_type=pl.DeviceIdType.MESH,
        )

    @pl.loop(1, count)
    def _(step):
        outgoing[step] = grads_ref[(me + step) % count].astype(jnp.bfloat16)

    pl.semaphore_wait(barrier, count - 1)

    @pl.loop(1, count)
    def _(step):
        piece(step).start()

    @pl.loop(1, count)
    def _(step):
        piece(step).wait()

    total = grads_ref[me]
    for step in range(1, count):
        total = total + arrived[step].astype(jnp.float32)
    summed[0] = total.astype(jnp.bfloat16)

    @pl.loop(1, count)
    def _(step):
        share(step).start()

    @pl.loop(1, count)
    def _(step):
        share(step).wait()

    @pl.loop(0, count)
    def _(step):
        total_ref[(me + count - step) % count] = summed[step].astype(jnp.float32)


def sum_over_devices(grads, col_count, row_count):
    count, rows, lanes = grads.shape
    vmem = pl.BlockSpec(memory_space=pltpu.VMEM)
    return pl.pallas_call(
        functools.partial(sum_kernel, col_count, row_count),
        out_shape=jax.ShapeDtypeStruct(grads.shape, grads.dtype),
        in_specs=[vmem],
        out_specs=vmem,
        scratch_shapes=[
            pltpu.VMEM((count, rows, lanes), jnp.bfloat16),
            pltpu.VMEM((count, rows, lanes), jnp.bfloat16),
            pltpu.VMEM((count, rows, lanes), jnp.bfloat16),
            pltpu.SemaphoreType.DMA((4, count)),
        ],
        compiler_params=pltpu.CompilerParams(collective_id=0, has_side_effects=True),
        name="sum_over_devices",
    )(grads)


def exchange_kernel(
    forward,
    col_count,
    row_count,
    left_ref,
    right_ref,
    left_out,
    right_out,
    left_sems,
    right_sems,
):
    group, col, row = lax.axis_index("groups"), lax.axis_index("col"), lax.axis_index("row")
    count = col_count * row_count
    me = col * row_count + row
    if forward:
        depth, part = left_ref.shape[0], left_ref.shape[1] // row_count
    else:
        depth, part = left_ref.shape[1] // row_count, left_ref.shape[2]

    def slab(index):
        return pl.ds(pl.multiple_of(index * depth, depth), depth)

    def cells(index):
        return pl.ds(pl.multiple_of(index * part, part), part)

    def left_ends(to_col, to_row):
        if forward:
            return left_ref.at[:, cells(to_row)], left_out.at[col, slab(row)]
        return left_ref.at[to_col, slab(to_row)], left_out.at[col, :, cells(row)]

    def right_ends(to_row):
        if forward:
            return right_ref, right_out.at[slab(row)]
        return right_ref.at[slab(to_row)], right_out.at[row]

    def send(ends, sems, step, to_col, to_row):
        return pltpu.make_async_remote_copy(
            src_ref=ends[0],
            dst_ref=ends[1],
            send_sem=sems.at[0, step],
            recv_sem=sems.at[1, step],
            device_id=(group, to_col, to_row),
            device_id_type=pl.DeviceIdType.MESH,
        )

    def left_copy(step):
        to = (me + step) % count
        to_col, to_row = to // row_count, to % row_count
        return send(left_ends(to_col, to_row), left_sems, step, to_col, to_row)

    def right_copy(step):
        to_row = (row + step) % row_count
        return send(right_ends(to_row), right_sems, step, col, to_row)

    barrier = pltpu.get_barrier_semaphore()

    @pl.loop(1, count)
    def _(step):
        to = (me + step) % count
        pl.semaphore_signal(
            barrier,
            inc=1,
            device_id=(group, to // row_count, to % row_count),
            device_id_type=pl.DeviceIdType.MESH,
        )

    own_left = pltpu.make_async_copy(*left_ends(col, row), left_sems.at[0, 0])
    own_right = pltpu.make_async_copy(*right_ends(row), right_sems.at[0, 0])
    own_left.start()
    own_right.start()
    pl.semaphore_wait(barrier, count - 1)

    @pl.loop(1, count)
    def _(step):
        left_copy(step).start()

    @pl.loop(1, row_count)
    def _(step):
        right_copy(step).start()

    own_left.wait()
    own_right.wait()

    @pl.loop(1, count)
    def _(step):
        left_copy(step).wait()

    @pl.loop(1, row_count)
    def _(step):
        right_copy(step).wait()


def exchange(forward, left, right, left_shape, right_shape, col_count, row_count):
    anywhere = pl.BlockSpec(memory_space=pl.ANY)
    return pl.pallas_call(
        functools.partial(exchange_kernel, forward, col_count, row_count),
        out_shape=(
            jax.ShapeDtypeStruct(left_shape, left.dtype),
            jax.ShapeDtypeStruct(right_shape, right.dtype),
        ),
        in_specs=[anywhere, anywhere],
        out_specs=(anywhere, anywhere),
        scratch_shapes=[
            pltpu.SemaphoreType.DMA((2, col_count * row_count)),
            pltpu.SemaphoreType.DMA((2, row_count)),
        ],
        compiler_params=pltpu.CompilerParams(
            collective_id=1 if forward else 2, has_side_effects=True
        ),
        name="gather_edges" if forward else "scatter_terms",
    )(left, right)


def body(
    pair_slab,
    tile_pair,
    tile_cotan,
    tile_rows,
    tile_count,
    norm_gain,
    norm_bias,
    w_in,
    out_gain,
    out_bias,
    w_out,
    w_gate,
):
    k_local, tile_len, channels = pair_slab.shape
    hidden_w = w_out.shape[0]
    slots = tile_rows.shape[1]
    row_count = lax.axis_size("row")
    col_count = lax.axis_size("col")
    row_part = tile_len // row_count
    slab_hat, slab_inv = normalize(pair_slab.astype(jnp.float32))
    slab_norm = (slab_hat * norm_gain + norm_bias).astype(jnp.bfloat16)
    flat_norm = slab_norm.reshape(-1, channels)
    project = jnp.dot(flat_norm, w_in, preferred_element_type=jnp.float32).reshape(
        k_local, tile_len, 4 * hidden_w
    )
    left_proj = project[..., :hidden_w]
    left_sig = jax.nn.sigmoid(project[..., hidden_w : 2 * hidden_w])
    right_proj = project[..., 2 * hidden_w : 3 * hidden_w]
    right_sig = jax.nn.sigmoid(project[..., 3 * hidden_w :])
    left_edges = (left_sig * left_proj).astype(jnp.bfloat16)
    right_edges = (right_sig * right_proj).astype(jnp.bfloat16)
    depth = k_local * row_count
    panels, right_full = exchange(
        True,
        left_edges,
        right_edges,
        (col_count, depth, row_part, hidden_w),
        (depth, tile_len, hidden_w),
        col_count,
        row_count,
    )
    update, pair_back, routed, right_part, out_total, gate_total = tile_work(
        tile_rows,
        tile_count,
        panels,
        right_full,
        tile_pair[0],
        tile_cotan[0],
        tuple(v[None, :] for v in (norm_gain, norm_bias, out_gain, out_bias)),
        w_out,
        w_gate,
    )
    left_terms, right_terms = exchange(
        False,
        routed,
        right_part,
        (col_count, k_local, tile_len, hidden_w),
        (row_count, k_local, tile_len, hidden_w),
        col_count,
        row_count,
    )
    left_grad = jnp.sum(left_terms.astype(jnp.float32), axis=0)
    right_grad = jnp.sum(right_terms.astype(jnp.float32), axis=0)
    grad_project = jnp.concatenate(
        [
            left_grad * left_sig,
            left_grad * left_proj * left_sig * (1.0 - left_sig),
            right_grad * right_sig,
            right_grad * right_proj * right_sig * (1.0 - right_sig),
        ],
        axis=-1,
    ).astype(jnp.bfloat16)
    flat_grad = grad_project.reshape(-1, 4 * hidden_w)
    grad_in_w = jnp.dot(flat_norm.T, flat_grad, preferred_element_type=jnp.float32)
    grad_norm = jnp.dot(flat_grad, w_in.T, preferred_element_type=jnp.float32).reshape(
        k_local, tile_len, channels
    )
    grad_slab = norm_back(grad_norm, slab_hat, slab_inv, norm_gain).astype(jnp.bfloat16)
    devices = row_count * col_count
    lanes = 128
    grads = [v.reshape(-1, lanes) for v in (grad_in_w, out_total, gate_total)]
    sizes = [v.shape[0] for v in grads]
    rows = -(-sum(sizes) // (16 * devices)) * 16
    spare = rows * devices - sum(sizes)
    grads = jnp.concatenate(grads + [jnp.zeros((spare, lanes), jnp.float32)] * (spare > 0))
    summed = sum_over_devices(grads.reshape(devices, rows, lanes), col_count, row_count)
    summed = summed.reshape(-1, lanes)
    in_total = summed[: sizes[0]].reshape(grad_in_w.shape)
    out_total = summed[sizes[0] : sizes[0] + sizes[1]].reshape(out_total.shape)
    gate_total = summed[sizes[0] + sizes[1] : sum(sizes)].reshape(gate_total.shape)
    update_out = update.reshape(1, slots, row_part, tile_len, channels)
    tiles_out = pair_back.reshape(1, slots, row_part, tile_len, channels)
    return (update_out, grad_slab, tiles_out, in_total, out_total, gate_total)


def solution(mesh):
    return jax.shard_map(
        body,
        mesh=mesh,
        in_specs=(
            P(("groups", "row"), "col", None),
            P(("groups", "col"), None, "row", None, None),
            P(("groups", "col"), None, "row", None, None),
            P(("groups", "col"), None),
            P(("groups", "col")),
            P(),
            P(),
            P(),
            P(),
            P(),
            P(),
            P(),
        ),
        out_specs=(
            P(("groups", "col"), None, "row", None, None),
            P(("groups", "row"), "col", None),
            P(("groups", "col"), None, "row", None, None),
            P("groups", None),
            P("groups", None),
            P("groups", None),
        ),
        check_vma=False,
    )
```
